256 devices in a mesh: expert: 128 (over z, x_hi, y, core), replica: 2 (over x_lo).
Axes of the slice: x: 4 (x_hi: 2, x_lo: 2; x = x_hi * 2 + x_lo), y: 4, z: 8, core: 2. Of those that a mesh axis runs over, the one named last changes fastest.
Arguments:
- tokens: bfloat16 [256, 256, 1280], P(('expert', 'replica')), may hold values from -20 to 20
- router: bfloat16 [1280, 128], replicated, may hold values from -0.41926275 to 0.41926275
- w_in: bfloat16 [128, 1280, 2560], P('expert', None, 'replica'), may hold values from -0.15625 to 0.15625
- w_out: bfloat16 [128, 2560, 1280], P('expert', 'replica'), may hold values from -0.125 to 0.125
- cotangent: bfloat16 [256, 256, 1280], P(('expert', 'replica')), may hold values from -6 to 6
Outputs:
- grad_tokens: bfloat16 [256, 256, 1280], P(('expert', 'replica'))
- grad_w_out: bfloat16 [128, 2560, 1280], P('expert', 'replica')
- grad_router: float32 [1280, 128], P('expert')
The draws below stay inside these ranges and needn't reach their ends.
All inputs are finite; a program needn't handle non-finite values.
Results may differ from the reference program's by a relative error of at most 0.019.
Values may be sent and summed in bfloat16 or wider, within the bound.
A program may use at most 128 MiB of HBM per device.

```python
import math
import jax
import jax.numpy as jnp
from jax import lax

D = 1280
FF = 2560
M = 256
EXPERTS = 128
IMAGES = 256


def draw_tokens(key, part):
    key = jax.random.fold_in(key, 11)
    keys = jax.random.split(key, 2)
    scales = jnp.exp(jax.random.uniform(keys[0], (IMAGES, M, 1), minval=math.log(0.3), maxval=math.log(3.0)))
    values = jnp.clip(jax.random.normal(keys[1], (IMAGES, M, D)), -6.0, 6.0) * scales
    return values.astype(jnp.bfloat16)


def draw_router(key, part):
    key = jax.random.fold_in(key, 12)
    keys = jax.random.split(key, 2)
    scales = jnp.exp(jax.random.uniform(keys[0], (1, EXPERTS), minval=math.log(0.5), maxval=math.log(2.5)))
    values = jnp.clip(jax.random.normal(keys[1], (D, EXPERTS)), -6.0, 6.0) * scales * D ** (-0.5)
    return values.astype(jnp.bfloat16)


def level_of(key, extent, shards, low, high):
    gain, own = 1.0, jax.random.fold_in(key, 6)
    for axis_at, parts in shards:
        steps = jnp.exp(jax.random.uniform(jax.random.fold_in(own, axis_at), (parts,), jnp.float32, low / len(shards), high / len(shards)))
        gain = gain * jnp.repeat(steps, extent[axis_at] // parts).reshape([-1 if axis == axis_at else 1 for axis in range(len(extent))])
    return gain


def centred(key, extent, scale, limit, pieces=(), kind=jnp.bfloat16):
    factor_of = level_of(key, extent, pieces, -0.22, 0.18) if pieces else 1.0
    drawn = jax.random.normal(key, extent, jnp.float32) * scale * factor_of
    return jnp.minimum(jnp.maximum(drawn, -limit), limit).astype(kind)


def setup_inputs(seed: int = 0) -> dict:
    key_list = jax.random.split(jax.random.key(seed), 6)
    return {
        "tokens": draw_tokens(jax.random.fold_in(key_list[5], 71), 0),
        "router": draw_router(jax.random.fold_in(key_list[5], 71), 0),
        "w_in": centred(key_list[2], (EXPERTS, D, FF), D ** -0.5, 0.15625, ((0, 128), (2, 2))),
        "w_out": centred(key_list[3], (EXPERTS, FF, D), FF ** -0.5, 0.125, ((0, 128), (1, 2))),
        "cotangent": centred(key_list[4], (IMAGES, M, D), 1.0, 6.0, ((0, 256),)),
    }


def gelu_slope(values):
    lower = 0.5 * (1.0 + lax.erf(values * 0.7071067811865476))
    return lower + values * jnp.exp(-0.5 * values * values) * 0.3989422804014327


def expert_pass(inputs):
    slot_rows, grad_rows, first_weight, second_weight = inputs
    pre_act = jnp.dot(slot_rows, first_weight, preferred_element_type=jnp.float32)
    hidden = jax.nn.gelu(pre_act, approximate=False).astype(jnp.bfloat16)
    slot_out = jnp.dot(hidden, second_weight, preferred_element_type=jnp.float32).astype(jnp.bfloat16)
    grad_hidden = jnp.dot(grad_rows, second_weight.T, preferred_element_type=jnp.float32)
    grad_pre = (grad_hidden * gelu_slope(pre_act)).astype(jnp.bfloat16)
    weight_grad = jnp.dot(hidden.T, grad_rows, preferred_element_type=jnp.float32).astype(jnp.bfloat16)
    grad_in = jnp.dot(grad_pre, first_weight.T, preferred_element_type=jnp.float32).astype(jnp.bfloat16)
    return slot_out, weight_grad, grad_in


def reference(tokens, router, w_in, w_out, cotangent):
    tok_wide = tokens.astype(jnp.float32)
    cot_wide = cotangent.astype(jnp.float32)
    router_wide = router.astype(jnp.float32)
    logits = jnp.einsum("imd,ds->ims", tok_wide, router_wide)
    dispatch = jax.nn.softmax(logits, axis=1)
    combine = jax.nn.softmax(logits, axis=2)
    dispatch_low = dispatch.astype(jnp.bfloat16)
    combine_low = combine.astype(jnp.bfloat16)
    slot_in = jnp.einsum("ims,imd->isd", dispatch_low.astype(jnp.float32), tok_wide).astype(jnp.bfloat16)
    grad_slot_out = jnp.einsum("ims,imd->isd", combine_low.astype(jnp.float32), cot_wide).astype(jnp.bfloat16)
    slot_out, grad_w_out, grad_slot_in = lax.map(
        expert_pass, (jnp.swapaxes(slot_in, 0, 1), jnp.swapaxes(grad_slot_out, 0, 1), w_in, w_out))
    slot_out = jnp.swapaxes(slot_out, 0, 1).astype(jnp.float32)
    grad_slot_in = jnp.swapaxes(grad_slot_in, 0, 1).astype(jnp.float32)
    grad_combine = jnp.einsum("imd,isd->ims", cot_wide, slot_out)
    grad_dispatch = jnp.einsum("imd,isd->ims", tok_wide, grad_slot_in)
    through_dispatch = dispatch * (grad_dispatch - jnp.sum(dispatch * grad_dispatch, axis=1, keepdims=True))
    through_combine = combine * (grad_combine - jnp.sum(combine * grad_combine, axis=2, keepdims=True))
    grad_logits = (through_dispatch + through_combine).astype(jnp.bfloat16).astype(jnp.float32)
    grad_tokens = (jnp.einsum("ims,isd->imd", dispatch_low.astype(jnp.float32), grad_slot_in)
                   + jnp.einsum("ims,ds->imd", grad_logits, router_wide)).astype(jnp.bfloat16)
    grad_router = jnp.einsum("imd,ims->ds", tok_wide, grad_logits)
    return grad_tokens, grad_w_out, grad_router
```

```python
import jax
import jax.numpy as jnp
from jax import lax
from jax.sharding import PartitionSpec as P


def gelu_slope(values):
    lower = 0.5 * (1.0 + lax.erf(values * 0.7071067811865476))
    return lower + values * jnp.exp(-0.5 * values * values) * 0.3989422804014327


def body(tokens, router, w_in, w_out, cotangent):
    width = tokens.shape[2]
    logits = jnp.einsum("imd,ds->ims", tokens, router, preferred_element_type=jnp.float32)
    dispatch = jax.nn.softmax(logits, axis=1)
    combine = jax.nn.softmax(logits, axis=2)
    dispatch_low = dispatch.astype(jnp.bfloat16)
    combine_low = combine.astype(jnp.bfloat16)
    slot_in = jnp.einsum(
        "ims,imd->isd", dispatch_low, tokens, preferred_element_type=jnp.float32
    ).astype(jnp.bfloat16)
    arrived = lax.all_to_all(slot_in, "expert", split_axis=1, concat_axis=0, tiled=True)
    slot_rows = arrived.reshape(-1, width)
    own_rows = slot_rows.shape[0]
    first_weight = w_in[0]
    second_weight = w_out[0]
    both_rows = lax.all_gather(slot_rows, "replica", axis=0, tiled=True)
    pre_act = jnp.dot(both_rows, first_weight, preferred_element_type=jnp.float32)
    hidden = jax.nn.gelu(pre_act, approximate=False).astype(jnp.bfloat16)
    picked = hidden
    slot_out = lax.psum_scatter(
        jnp.dot(picked, second_weight, preferred_element_type=jnp.float32).astype(jnp.bfloat16),
        "replica",
        scatter_dimension=0,
        tiled=True,
    )
    returned = lax.all_to_all(
        slot_out.reshape(own_rows, 1, width), "expert", split_axis=0, concat_axis=1, tiled=True
    )
    grad_slot_out = jnp.einsum(
        "ims,imd->isd", combine_low, cotangent, preferred_element_type=jnp.float32
    ).astype(jnp.bfloat16)
    grad_combine = jnp.einsum(
        "imd,isd->ims", cotangent, returned, preferred_element_type=jnp.float32
    )
    grad_arrived = lax.all_to_all(grad_slot_out, "expert", split_axis=1, concat_axis=0, tiled=True)
    grad_rows = grad_arrived.reshape(-1, width)
    both_grads = lax.all_gather(grad_rows, "replica", axis=0, tiled=True)
    grad_hidden = jnp.einsum(
        "rd,fd->rf", both_grads, second_weight, preferred_element_type=jnp.float32
    )
    grad_pre = (grad_hidden * gelu_slope(pre_act)).astype(jnp.bfloat16)
    grad_second = jnp.einsum(
        "rf,rd->fd", hidden, both_grads, preferred_element_type=jnp.float32
    ).astype(jnp.bfloat16)
    picked = grad_pre
    grad_slot_in = lax.psum_scatter(
        jnp.einsum("rf,df->rd", picked, first_weight, preferred_element_type=jnp.float32).astype(
            jnp.bfloat16
        ),
        "replica",
        scatter_dimension=0,
        tiled=True,
    )
    grad_back = lax.all_to_all(
        grad_slot_in.reshape(own_rows, 1, width), "expert", split_axis=0, concat_axis=1, tiled=True
    )
    grad_dispatch = jnp.einsum(
        "imd,isd->ims", tokens, grad_back, preferred_element_type=jnp.float32
    )
    through_dispatch = dispatch * (
        grad_dispatch - jnp.sum(dispatch * grad_dispatch, axis=1, keepdims=True)
    )
    through_combine = combine * (
        grad_combine - jnp.sum(combine * grad_combine, axis=2, keepdims=True)
    )
    grad_logits = (through_dispatch + through_combine).astype(jnp.bfloat16)
    grad_tokens = (
        jnp.einsum("ims,isd->imd", dispatch_low, grad_back, preferred_element_type=jnp.float32)
        + jnp.einsum("ims,ds->imd", grad_logits, router, preferred_element_type=jnp.float32)
    ).astype(jnp.bfloat16)
    router_term = jnp.einsum("imd,ims->ds", tokens, grad_logits, preferred_element_type=jnp.float32)
    shares = lax.all_to_all(
        router_term.astype(jnp.bfloat16).reshape(128, -1, router_term.shape[1]),
        "expert", split_axis=0, concat_axis=0, tiled=True,
    )
    group_sum = jnp.sum(shares.astype(jnp.float32), axis=0)
    grad_router = lax.psum(group_sum, "replica")
    return (grad_tokens, grad_second[None], grad_router)


def solution(mesh):
    placed = (
        P(("expert", "replica"), None, None),
        P(),
        P("expert", None, "replica"),
        P("expert", "replica", None),
        P(("expert", "replica"), None, None),
    )
    return jax.shard_map(
        body,
        mesh=mesh,
        in_specs=placed,
        out_specs=(
            P(("expert", "replica"), None, None),
            P("expert", "replica", None),
            P("expert", None),
        ),
        check_vma=False,
    )
```

```python
import functools

import jax
import jax.numpy as jnp
from jax import lax
from jax.experimental import pallas as pl
from jax.experimental.pallas import tpu as pltpu
from jax.sharding import PartitionSpec as P

F32 = jnp.float32
BF16 = jnp.bfloat16
MESH = pl.DeviceIdType.MESH
PLANE = 16


def tile_of(width):
    return 256 if width % 256 == 0 else width


def matmul(a, b):
    return jnp.dot(a, b, preferred_element_type=F32)


def matmul_nt(a, b):
    return lax.dot_general(a, b, (((1,), (1,)), ((), ())), preferred_element_type=F32)


def matmul_tn(a, b):
    return lax.dot_general(a, b, (((0,), (0,)), ((), ())), preferred_element_type=F32)


def softmax(logits, axis):
    raised = jnp.exp(logits - jnp.max(logits, axis=axis, keepdims=True))
    return raised / jnp.sum(raised, axis=axis, keepdims=True)


def kernel(
    nz, np_, share, pad,
    tok_hbm, rt_hbm, win_hbm, wout_hbm, cot_hbm,
    gt_hbm, gw_hbm, gr_ref,
    tok, rt, win, wout, cot, tok_t,
    disp, comb, through,
    slots, gathered, bundles, arrived, rows,
    hid, slope, gpre, wide, partial, partials, sent_back, returned,
    rsend, rmid, rpad, rall, gw, gt,
    load_sem, store_sem, zs_sem, zr_sem, ps_sem, pr_sem,
):
    e = lax.axis_index("expert")
    r = lax.axis_index("replica")
    z = lax.div(e, np_)
    p = lax.rem(e, np_)
    nq = 2 * np_
    q = r * np_ + p
    experts = nz * np_
    width = tok.shape[1]
    half = width // 2
    inner = hid.shape[1]

    def z_peer(k):
        other = lax.rem(z + k, nz)
        return other, (other * np_ + p, r)

    def z_source(k):
        return lax.rem(z + nz - k, nz)

    def plane_peer(k):
        other = lax.rem(q + k, nq)
        return other, (z * np_ + lax.rem(other, np_), lax.div(other, np_))

    def plane_source(k):
        return lax.rem(q + nq - k, nq)

    barrier = pltpu.get_barrier_semaphore()

    @pl.loop(1, nz)
    def _(k):
        pl.semaphore_signal(barrier, inc=1, device_id=z_peer(k)[1], device_id_type=MESH)

    @pl.loop(1, nq)
    def _(k):
        pl.semaphore_signal(barrier, inc=1, device_id=plane_peer(k)[1], device_id_type=MESH)

    loads = [
        pltpu.make_async_copy(src, dst, load_sem.at[i])
        for i, (src, dst) in enumerate(
            ((tok_hbm, tok), (rt_hbm, rt), (cot_hbm, cot), (win_hbm, win), (wout_hbm, wout)))
    ]
    for load in loads:
        load.start()

    def z_copy(i, src, dst, k, at):
        other, device = z_peer(k)
        return pltpu.make_async_remote_copy(
            src_ref=src.at[other], dst_ref=dst.at[at], send_sem=zs_sem.at[i, k],
            recv_sem=zr_sem.at[i, k], device_id=device, device_id_type=MESH)

    def z_send(i, src, dst):
        @pl.loop(1, nz)
        def _(k):
            z_copy(i, src, dst, k, z).start()
        dst[z] = src[z]

    def z_wait(i, src, dst):
        @pl.loop(1, nz)
        def _(k):
            z_copy(i, src, dst, k, z_source(k)).wait_recv()

    def z_drain(i, src, dst):
        @pl.loop(1, nz)
        def _(k):
            z_copy(i, src, dst, k, z).wait_send()

    def plane_copy(i, src, dst, k, at, fold):
        other, device = plane_peer(k)
        return pltpu.make_async_remote_copy(
            src_ref=src.at[lax.rem(other, np_) if fold else other], dst_ref=dst.at[at],
            send_sem=ps_sem.at[i, k], recv_sem=pr_sem.at[i, k],
            device_id=device, device_id_type=MESH)

    def plane_send(i, src, dst, fold):
        @pl.loop(1, nq)
        def _(k):
            plane_copy(i, src, dst, k, q, fold).start()
        dst[q] = src[p if fold else q]

    def plane_wait(i, src, dst, fold):
        @pl.loop(1, nq)
        def _(k):
            plane_copy(i, src, dst, k, plane_source(k), fold).wait_recv()

    def plane_drain(i, src, dst, fold):
        @pl.loop(1, nq)
        def _(k):
            plane_copy(i, src, dst, k, q, fold).wait_send()

    loads[0].wait()
    loads[1].wait()
    logits = matmul(tok[...], rt[...])
    dispatch = softmax(logits, 0)
    disp[...] = dispatch
    slots[0] = matmul(dispatch.T.astype(BF16), tok[...]).astype(BF16).reshape(nz, np_, width)
    pl.semaphore_wait(barrier, nz - 1 + nq - 1)
    z_send(0, slots.at[0], gathered.at[0])
    combine = softmax(logits, 1)
    comb[...] = combine
    loads[2].wait()
    slots[1] = matmul(combine.T.astype(BF16), cot[...]).astype(BF16).reshape(nz, np_, width)
    z_send(1, slots.at[1], gathered.at[1])
    tok_t[...] = tok[...].T

    span = 2 * nz
    at_row = lax.broadcasted_iota(jnp.int32, (np_ * span, experts), 0)
    at_col = lax.broadcasted_iota(jnp.int32, (np_ * span, experts), 1)
    spread = [
        jnp.where(
            at_row == lax.rem(at_col, np_) * span + h * nz + lax.div(at_col, np_), 1.0, 0.0
        ).astype(BF16)
        for h in range(2)
    ]
    for i in range(2):
        z_wait(i, slots.at[i], gathered.at[i])
        block = gathered[i].reshape(experts, width)
        bundles[i] = (
            matmul(spread[0], block[:, :half]) + matmul(spread[1], block[:, half:])
        ).astype(BF16).reshape(np_, span, half)
        plane_send(2 * i, bundles.at[i], arrived.at[i], True)

    def unbundle(i):
        plane_wait(2 * i, bundles.at[i], arrived.at[i], True)
        block = arrived[i].astype(F32)
        for h in range(2):
            rows[i, :, h * half:(h + 1) * half] = (
                block[:, h * nz:(h + 1) * nz, :].reshape(nq * nz, half).astype(BF16))

    def bundle(i):
        partial[i] = wide[...].astype(BF16)
        plane_send(2 * i + 1, partial.at[i], partials.at[i], False)

    step = tile_of(inner)
    unbundle(0)
    loads[3].wait()

    @pl.loop(0, inner // step)
    def _(t):
        at = pl.ds(pl.multiple_of(t * step, step), step)
        pre = matmul(rows[0], win[:, at])
        lower = 0.5 * (1.0 + lax.erf(pre * 0.7071067811865476))
        hid[:, at] = (pre * lower).astype(BF16)
        slope[:, at] = lower + pre * jnp.exp(-0.5 * pre * pre) * 0.3989422804014327

    loads[4].wait()
    for h in range(2):
        wide[:, h * nz:(h + 1) * nz, :] = matmul(
            hid[...], wout[:, h * half:(h + 1) * half]).reshape(nq, nz, half)
    bundle(0)

    unbundle(1)

    @pl.loop(0, inner // step)
    def _(t):
        at = pl.ds(pl.multiple_of(t * step, step), step)
        gpre[:, at] = (matmul_nt(rows[1], wout[at, :]) * slope[:, at]).astype(BF16)

    for h in range(2):
        wide[:, h * nz:(h + 1) * nz, :] = matmul_nt(
            gpre[...], win[h * half:(h + 1) * half, :]).reshape(nq, nz, half)
    bundle(1)

    def gateway_back(i):
        plane_wait(2 * i + 1, partial.at[i], partials.at[i], False)
        both = (partials[i, :np_].astype(F32) + partials[i, np_:].astype(F32)).astype(BF16)
        both = both.reshape(np_ * span, half)
        for h in range(2):
            sent_back[i, :, :, h * half:(h + 1) * half] = matmul_tn(
                spread[h], both).astype(BF16).reshape(nz, np_, half)
        z_send(2 + i, sent_back.at[i], returned.at[i])

    gateway_back(0)

    @pl.loop(0, inner // step)
    def _(t):
        at = pl.ds(pl.multiple_of(t * step, step), step)
        gw[at, :] = matmul_tn(hid[:, at], rows[1]).astype(BF16)

    store_gw = pltpu.make_async_copy(gw, gw_hbm, store_sem.at[0])
    store_gw.start()
    gateway_back(1)

    z_wait(2, sent_back.at[0], returned.at[0])
    grad_combine = matmul_nt(cot[...], returned[0].reshape(experts, width))
    weight = comb[...]
    through[...] = weight * (
        grad_combine - jnp.sum(weight * grad_combine, axis=1, keepdims=True))
    z_wait(3, sent_back.at[1], returned.at[1])
    grad_rows = returned[1].reshape(experts, width)
    grad_dispatch = matmul_nt(tok[...], grad_rows)
    weight = disp[...]
    grad_logits = (
        weight * (grad_dispatch - jnp.sum(weight * grad_dispatch, axis=0, keepdims=True))
        + through[...]
    ).astype(BF16)
    rsend[...] = matmul(tok_t[...], grad_logits).astype(BF16).reshape(rsend.shape)
    z_send(4, rsend, rmid)
    gt[...] = (
        matmul(weight.astype(BF16), grad_rows) + matmul_nt(grad_logits, rt[...])
    ).astype(BF16)
    store_gt = pltpu.make_async_copy(gt, gt_hbm, store_sem.at[1])
    store_gt.start()
    z_wait(4, rsend, rmid)
    group = rmid[0].astype(F32)
    for k in range(1, nz):
        group = group + rmid[k].astype(F32)
    at_row = lax.broadcasted_iota(jnp.int32, (np_ * pad, np_ * share), 0)
    at_col = lax.broadcasted_iota(jnp.int32, (np_ * pad, np_ * share), 1)
    own = lax.rem(at_row, pad)
    place = jnp.where(
        (at_col == lax.div(at_row, pad) * share + own) & (own < share), 1.0, 0.0).astype(BF16)
    rpad[...] = matmul(place, group.astype(BF16)).astype(BF16).reshape(rpad.shape)
    plane_send(4, rpad, rall, True)
    plane_wait(4, rpad, rall, True)
    total = jnp.sum(rall[...].astype(F32), axis=0)
    gr_ref[...] = total[:share]

    for i in range(2):
        z_drain(i, slots.at[i], gathered.at[i])
        z_drain(2 + i, sent_back.at[i], returned.at[i])
        plane_drain(2 * i, bundles.at[i], arrived.at[i], True)
        plane_drain(2 * i + 1, partial.at[i], partials.at[i], False)
    z_drain(4, rsend, rmid)
    plane_drain(4, rpad, rall, True)
    store_gw.wait()
    store_gt.wait()


def body(np_, tokens, router, w_in, w_out, cotangent):
    tokens, cotangent, w_in, w_out = tokens[0], cotangent[0], w_in[0], w_out[0]
    count, width = tokens.shape
    experts = router.shape[1]
    inner = w_in.shape[1]
    nz = experts // np_
    nq = 2 * np_
    span = 2 * nz
    half = width // 2
    share = width // experts
    pad = -(-share // 16) * 16
    vm = pltpu.VMEM
    anywhere = pl.BlockSpec(memory_space=pl.ANY)
    gt, gw, gr = pl.pallas_call(
        functools.partial(kernel, nz, np_, share, pad),
        out_shape=(
            jax.ShapeDtypeStruct((count, width), BF16),
            jax.ShapeDtypeStruct((inner, width), BF16),
            jax.ShapeDtypeStruct((share, experts), F32),
        ),
        in_specs=[anywhere] * 5,
        out_specs=(anywhere, anywhere, pl.BlockSpec(memory_space=pltpu.VMEM)),
        scratch_shapes=[
            vm((count, width), BF16), vm(router.shape, BF16), vm(w_in.shape, BF16),
            vm(w_out.shape, BF16), vm((count, width), BF16), vm((width, count), BF16),
            vm((count, experts), F32), vm((count, experts), F32), vm((count, experts), F32),
            vm((2, nz, np_, width), BF16), vm((2, nz, np_, width), BF16),
            vm((2, np_, span, half), BF16), vm((2, nq, span, half), BF16),
            vm((2, nq * nz, width), BF16),
            vm((nq * nz, inner), BF16), vm((nq * nz, inner), F32), vm((nq * nz, inner), BF16),
            vm((nq, span, half), F32), vm((2, nq, span, half), BF16),
            vm((2, nq, span, half), BF16),
            vm((2, nz, np_, width), BF16), vm((2, nz, np_, width), BF16),
            vm((nz, np_ * share, experts), BF16), vm((nz, np_ * share, experts), BF16),
            vm((np_, pad, experts), BF16), vm((nq, pad, experts), BF16),
            vm((inner, width), BF16), vm((count, width), BF16),
            pltpu.SemaphoreType.DMA((5,)), pltpu.SemaphoreType.DMA((2,)),
            pltpu.SemaphoreType.DMA((5, nz)), pltpu.SemaphoreType.DMA((5, nz)),
            pltpu.SemaphoreType.DMA((5, nq)), pltpu.SemaphoreType.DMA((5, nq)),
        ],
        compiler_params=pltpu.CompilerParams(
            collective_id=0, has_side_effects=True, vmem_limit_bytes=50 * 1024 * 1024),
    )(tokens, router, w_in, w_out, cotangent)
    return gt[None], gw[None], gr


def solution(mesh, plane=PLANE):
    placed = (
        P(("expert", "replica"), None, None),
        P(),
        P("expert", None, "replica"),
        P("expert", "replica", None),
        P(("expert", "replica"), None, None),
    )
    return jax.shard_map(
        functools.partial(body, plane),
        mesh=mesh,
        in_specs=placed,
        out_specs=(
            P(("expert", "replica"), None, None),
            P("expert", "replica", None),
            P("expert", None),
        ),
        check_vma=False,
    )
```

```python
import functools

import jax
import jax.numpy as jnp
from jax import lax
from jax.experimental import pallas as pl
from jax.experimental.pallas import tpu as pltpu
from jax.sharding import PartitionSpec as P

F32 = jnp.float32
BF16 = jnp.bfloat16
MESH = pl.DeviceIdType.MESH
PLANE = 16
COLUMNS = 256


def matmul(a, b):
    return jnp.dot(a, b, preferred_element_type=F32)


def matmul_nt(a, b):
    return lax.dot_general(a, b, (((1,), (1,)), ((), ())), preferred_element_type=F32)


def matmul_tn(a, b):
    return lax.dot_general(a, b, (((0,), (0,)), ((), ())), preferred_element_type=F32)


def softmax(logits, axis):
    raised = jnp.exp(logits - jnp.max(logits, axis=axis, keepdims=True))
    return raised / jnp.sum(raised, axis=axis, keepdims=True)


def kernel(
    nz, np_, share, cols, pad, tall,
    tok_hbm, rt_hbm, win_hbm, wout_hbm, cot_hbm,
    gt, gw, gr,
    tok, rt, win, wout, cot, tok_p,
    disp, comb, disp_t, comb_t, grad_c, grad_d,
    slots, gathered, bundles, arrived, partial, partials, sent_back, returned,
    regroup, regroup_t, xb, pre, gh, hid, gpre, grad_rows,
    rsend, rall, rpart, rfin,
    load_sem, fz_s, fz_r, fp_s, fp_r, bp_s, bp_r, bz_s, bz_r, rp_s, rp_r, rf_s, rf_r,
):
    e = lax.axis_index("expert")
    r = lax.axis_index("replica")
    z = lax.div(e, np_)
    p = lax.rem(e, np_)
    nq = 2 * np_
    q = r * np_ + p
    experts = nz * np_
    span = 2 * nz
    wide = 2 * np_
    width = tok.shape[1]
    inner = hid.shape[1]
    chunks = width // cols
    step = 256 if inner % 256 == 0 else inner
    tiles = inner // step
    upper = nz // 2

    def z_peer(k):
        far = lax.div(k + 1, 2)
        far = far + (1 - lax.rem(k, 2)) * (nz - 2 * far)
        return lax.rem(z + far, nz)

    def plane_peer(k):
        return lax.rem(q + k, nq)

    def plane_device(other):
        return (z * np_ + lax.rem(other, np_), lax.div(other, np_))

    loads = [
        pltpu.make_async_copy(src, dst, load_sem.at[i])
        for i, (src, dst) in enumerate(
            ((tok_hbm, tok), (rt_hbm, rt), (cot_hbm, cot), (win_hbm, win), (wout_hbm, wout)))
    ]
    for load in loads:
        load.start()

    barrier = pltpu.get_barrier_semaphore()

    @pl.loop(1, nz)
    def _(k):
        other = z_peer(k) * np_ + p
        pl.semaphore_signal(barrier, inc=1, device_id=(other, r), device_id_type=MESH)
        pl.semaphore_signal(barrier, inc=1, device_id=(other, 1 - r), device_id_type=MESH)

    @pl.loop(1, nq)
    def _(k):
        pl.semaphore_signal(
            barrier, inc=1, device_id=plane_device(plane_peer(k)), device_id_type=MESH)

    def z_send(src, dst, s, t):
        @pl.loop(1, nz)
        def _(k):
            other = z_peer(k)
            pltpu.make_async_remote_copy(
                src_ref=src.at[other], dst_ref=dst.at[z], send_sem=s, recv_sem=t,
                device_id=(other * np_ + p, r), device_id_type=MESH).start()
        dst[z] = src[z]

    def plane_send(src, dst, s, t, fold):
        @pl.loop(1, nq)
        def _(k):
            other = plane_peer(k)
            pltpu.make_async_remote_copy(
                src_ref=src.at[lax.rem(other, np_) if fold else other], dst_ref=dst.at[q],
                send_sem=s, recv_sem=t, device_id=plane_device(other),
                device_id_type=MESH).start()
        dst[q] = src[p if fold else q]

    def all_of(ref, count, s, t):
        part = ref.at[pl.ds(0, count)]
        return pltpu.make_async_remote_copy(
            src_ref=part, dst_ref=part, send_sem=s, recv_sem=t,
            device_id=plane_device(plane_peer(1)), device_id_type=MESH)

    def columns(c):
        return pl.ds(pl.multiple_of(c * cols, cols), cols)

    def hidden_units(t):
        return pl.ds(pl.multiple_of(t * step, step), step)

    pre[...] = jnp.zeros_like(pre)
    gh[...] = jnp.zeros_like(gh)
    grad_c[...] = jnp.zeros_like(grad_c)
    grad_d[...] = jnp.zeros_like(grad_d)
    loads[0].wait()
    loads[1].wait()
    logits = matmul(tok[...], rt[...])
    dispatch = softmax(logits, 0)
    disp[...] = dispatch
    disp_t[...] = dispatch.T.astype(BF16)
    combine = softmax(logits, 1)
    comb[...] = combine
    comb_t[...] = combine.T.astype(BF16)
    loads[2].wait()
    pl.semaphore_wait(barrier, 2 * (nz - 1) + nq - 1)

    @pl.loop(0, chunks)
    def _(c):
        at = columns(c)
        slots[c, :, :np_, :] = matmul(disp_t[...], tok[:, at]).astype(BF16).reshape(
            nz, np_, cols)
        slots[c, :, np_:, :] = matmul(comb_t[...], cot[:, at]).astype(BF16).reshape(
            nz, np_, cols)
        z_send(slots.at[c], gathered.at[c], fz_s.at[c], fz_r.at[c])

    at_row = lax.broadcasted_iota(jnp.int32, (np_ * span, nz * wide), 0)
    at_col = lax.broadcasted_iota(jnp.int32, (np_ * span, nz * wide), 1)
    inside = lax.rem(at_col, wide)
    regroup[...] = jnp.where(
        at_row == lax.rem(inside, np_) * span + lax.div(inside, np_) * nz
        + lax.div(at_col, wide), 1.0, 0.0).astype(BF16)
    inside = lax.rem(at_row, wide)
    regroup_t[...] = jnp.where(
        at_col == lax.rem(inside, np_) * span + lax.div(inside, np_) * nz
        + lax.div(at_row, wide), 1.0, 0.0).astype(BF16)

    def gateway(c):
        all_of(gathered.at[c], nz - 1, fz_s.at[c], fz_r.at[c]).wait_recv()
        bundles[c] = matmul(
            regroup[...], gathered[c].reshape(nz * wide, cols)
        ).astype(BF16).reshape(np_, span, cols)
        plane_send(bundles.at[c], arrived.at[c], fp_s.at[c], fp_r.at[c], True)

    many = tok_p.shape[0] // 4

    def spread_tokens(t):
        row = lax.broadcasted_iota(jnp.int32, (many, width), 0) + t * many
        col = lax.broadcasted_iota(jnp.int32, (many, width), 1)
        to = lax.div(row, tall)
        row = row - to * tall
        level = jnp.zeros_like(row)
        for k in range(1, upper):
            level = level + jnp.where(row >= k * share, 1, 0)
        level_r = lax.div(to, np_)
        source = (
            (level_r * upper + level) * (np_ * share) + (to - level_r * np_) * share
            + row - level * share)
        pick = jnp.where((col == source) & (row < upper * share), 1.0, 0.0).astype(BF16)
        tok_p[pl.ds(pl.multiple_of(t * many, many), many), :] = matmul_nt(
            pick, tok[...]).astype(BF16)

    def expert_rows(c):
        all_of(arrived.at[c], nq - 1, fp_s.at[c], fp_r.at[c]).wait_recv()
        block = arrived[c].astype(F32)
        xa = block[:, :nz, :].reshape(nq * nz, cols).astype(BF16)
        own = block[:, nz:, :].reshape(nq * nz, cols).astype(BF16)
        xb[:, columns(c)] = own
        return xa, own

    def accumulate(c):
        xa, own = expert_rows(c)

        @pl.loop(0, tiles)
        def _(t):
            at = hidden_units(t)
            pre[:, at] += matmul(xa, win[columns(c), at])
            gh[:, at] += matmul_nt(own, wout[at, columns(c)])

    lag = min(2, chunks - 1)

    @pl.loop(0, lag)
    def _(c):
        gateway(c)
        spread_tokens(2 * c)
        spread_tokens(2 * c + 1)

    if lag == 1:
        spread_tokens(2)
        spread_tokens(3)
    loads[3].wait()
    loads[4].wait()

    @pl.loop(lag, chunks)
    def _(c):
        gateway(c)
        accumulate(c - lag)

    @pl.loop(chunks - lag, chunks - 1)
    def _(c):
        accumulate(c)

    last = chunks - 1
    xa, own = expert_rows(last)

    @pl.loop(0, tiles)
    def _(t):
        at = hidden_units(t)
        act = pre[:, at] + matmul(xa, win[columns(last), at])
        lower = 0.5 * (1.0 + lax.erf(act * 0.7071067811865476))
        hid[:, at] = (act * lower).astype(BF16)
        slope = lower + act * jnp.exp(-0.5 * act * act) * 0.3989422804014327
        grad = gh[:, at] + matmul_nt(own, wout[at, columns(last)])
        gpre[:, at] = (grad * slope).astype(BF16)

    @pl.loop(0, chunks)
    def _(c):
        at = columns(c)
        out = matmul(hid[...], wout[:, at]).reshape(nq, nz, cols)
        back = matmul_nt(gpre[...], win[at, :]).reshape(nq, nz, cols)
        partial[c] = jnp.concatenate([out, back], axis=1).astype(BF16)
        plane_send(partial.at[c], partials.at[c], bp_s.at[c], bp_r.at[c], False)

    def gateway_back(c):
        all_of(partials.at[c], nq - 1, bp_s.at[c], bp_r.at[c]).wait_recv()
        both = (partials[c, :np_].astype(F32) + partials[c, np_:].astype(F32)).astype(BF16)
        sent_back[c] = matmul(
            regroup_t[...], both.reshape(np_ * span, cols)
        ).astype(BF16).reshape(nz, wide, cols)
        z_send(sent_back.at[c], returned.at[c], bz_s.at[c], bz_r.at[c])

    def image_rows(c):
        all_of(returned.at[c], nz - 1, bz_s.at[c], bz_r.at[c]).wait_recv()
        at = columns(c)
        block = returned[c]
        grad_c[...] += matmul_nt(cot[:, at], block[:, :np_, :].reshape(experts, cols))
        own = block[:, np_:, :].reshape(experts, cols)
        grad_rows[:, at] = own
        grad_d[...] += matmul_nt(tok[:, at], own)

    def weight_rows(t):
        at = hidden_units(t)
        gw[at, :] = matmul_tn(hid[:, at], xb[...]).astype(BF16)

    def forward_sent(c):
        all_of(slots.at[c], nz - 1, fz_s.at[c], fz_r.at[c]).wait_send()
        all_of(arrived.at[c], nq - 1, fp_s.at[c], fp_r.at[c]).wait_send()

    @pl.loop(0, tiles)
    def _(t):
        weight_rows(t)

    @pl.loop(0, lag)
    def _(c):
        gateway_back(c)
        forward_sent(c)

    @pl.loop(lag, chunks)
    def _(c):
        gateway_back(c)
        forward_sent(c)
        image_rows(c - lag)

    @pl.loop(chunks - lag, chunks)
    def _(c):
        image_rows(c)

    got = grad_c[...]
    weight = comb[...]
    through = weight * (got - jnp.sum(weight * got, axis=1, keepdims=True))
    got = grad_d[...]
    weight = disp[...]
    grad_logits = (
        weight * (got - jnp.sum(weight * got, axis=0, keepdims=True)) + through
    ).astype(BF16)
    rsend[...] = matmul(tok_p[...], grad_logits).astype(BF16).reshape(rsend.shape)
    plane_send(rsend, rall, rp_s, rp_r, False)
    gt[...] = (
        matmul(weight.astype(BF16), grad_rows[...]) + matmul_nt(grad_logits, rt[...])
    ).astype(BF16)

    @pl.loop(0, chunks)
    def _(c):
        all_of(partials.at[c], nq - 1, bp_s.at[c], bp_r.at[c]).wait_send()
        all_of(returned.at[c], nz - 1, bz_s.at[c], bz_r.at[c]).wait_send()

    at_row = lax.broadcasted_iota(jnp.int32, (upper * pad, tall), 0)
    at_col = lax.broadcasted_iota(jnp.int32, (upper * pad, tall), 1)
    level = lax.div(at_row, pad)
    own = at_row - level * pad
    place = jnp.where(
        (at_col == level * share + own) & (own < share), 1.0, 0.0).astype(BF16)
    all_of(rall, nq - 1, rp_s, rp_r).wait_recv()
    group = jnp.sum(rall[...].astype(F32), axis=0).astype(BF16)
    rpart[...] = matmul(place, group).astype(BF16).reshape(rpart.shape)
    mine = lax.div(z, upper)

    def hand_over(t):
        level, other = lax.div(t, 2), lax.rem(t, 2)
        to = r * upper + level
        copy = pltpu.make_async_remote_copy(
            src_ref=rpart.at[level], dst_ref=rfin.at[z], send_sem=rf_s.at[t],
            recv_sem=rf_r.at[z], device_id=(to * np_ + p, other), device_id_type=MESH)
        return copy, (to != z) | (other != r)

    @pl.loop(0, nz)
    def _(t):
        copy, away = hand_over(t)

        @pl.when(away)
        def _():
            copy.start()

        @pl.when(jnp.logical_not(away))
        def _():
            rfin[z] = rpart[lax.div(t, 2)]

    @pl.loop(0, nz)
    def _(k):
        @pl.when((k != z) | (mine != r))
        def _():
            pltpu.make_async_remote_copy(
                src_ref=rpart.at[0], dst_ref=rfin.at[k], send_sem=rf_s.at[0],
                recv_sem=rf_r.at[k], device_id=plane_device(plane_peer(1)),
                device_id_type=MESH).wait_recv()

    gr[...] = jnp.sum(rfin[...].astype(F32), axis=0)[:share]
    all_of(rsend, nq - 1, rp_s, rp_r).wait_send()

    @pl.loop(0, nz)
    def _(t):
        copy, away = hand_over(t)

        @pl.when(away)
        def _():
            copy.wait_send()


def write_out(gt, gw, gr, gt_hbm, gw_hbm, gr_hbm, sem):
    moves = [
        pltpu.make_async_copy(src, dst, sem.at[i])
        for i, (src, dst) in enumerate(((gw, gw_hbm), (gt, gt_hbm), (gr, gr_hbm)))
    ]
    for move in moves:
        move.start()
    for move in moves:
        move.wait()


def body(np_, cols, tokens, router, w_in, w_out, cotangent):
    count, width = tokens.shape[1:]
    experts = router.shape[1]
    inner = w_in.shape[2]
    nz = experts // np_
    nq = 2 * np_
    span = 2 * nz
    wide = 2 * np_
    share = width // experts
    pad = -(-share // 16) * 16
    tall = -(-share * (nz // 2) // 16) * 16
    chunks = width // cols
    vm = pltpu.VMEM
    dma = pltpu.SemaphoreType.DMA
    whole = pl.BlockSpec(memory_space=vm)
    far = pl.BlockSpec(memory_space=pltpu.HBM)
    operands = [
        pltpu.with_memory_space_constraint(a, pltpu.HBM)
        for a in (tokens[0], router, w_in[0], w_out[0], cotangent[0])
    ]
    outs = pl.pallas_call(
        functools.partial(kernel, nz, np_, share, cols, pad, tall),
        out_shape=(vm((count, width), BF16), vm((inner, width), BF16), vm((share, experts), F32)),
        in_specs=[far] * 5,
        out_specs=(whole, whole, whole),
        scratch_shapes=[
            vm((count, width), BF16), vm(router.shape, BF16), vm((width, inner), BF16),
            vm((inner, width), BF16), vm((count, width), BF16), vm((nq * tall, count), BF16),
            vm((count, experts), F32), vm((count, experts), F32),
            vm((experts, count), BF16), vm((experts, count), BF16),
            vm((count, experts), F32), vm((count, experts), F32),
            vm((chunks, nz, wide, cols), BF16), vm((chunks, nz, wide, cols), BF16),
            vm((chunks, np_, span, cols), BF16), vm((chunks, nq, span, cols), BF16),
            vm((chunks, nq, span, cols), BF16), vm((chunks, nq, span, cols), BF16),
            vm((chunks, nz, wide, cols), BF16), vm((chunks, nz, wide, cols), BF16),
            vm((np_ * span, nz * wide), BF16), vm((nz * wide, np_ * span), BF16),
            vm((nq * nz, width), BF16), vm((nq * nz, inner), F32), vm((nq * nz, inner), F32),
            vm((nq * nz, inner), BF16), vm((nq * nz, inner), BF16), vm((experts, width), BF16),
            vm((nq, tall, experts), BF16), vm((nq, tall, experts), BF16),
            vm((nz // 2, pad, experts), BF16), vm((nz, pad, experts), BF16),
            dma((5,)), dma((chunks,)), dma((chunks,)), dma((chunks,)), dma((chunks,)),
            dma((chunks,)), dma((chunks,)), dma((chunks,)), dma((chunks,)),
            dma(()), dma(()), dma((nz,)), dma((nz,)),
        ],
        compiler_params=pltpu.CompilerParams(
            collective_id=0, has_side_effects=True, vmem_limit_bytes=48 * 1024 * 1024),
    )(*operands)
    gt, gw, gr = pl.pallas_call(
        write_out,
        out_shape=[jax.ShapeDtypeStruct(a.shape, a.dtype) for a in outs],
        in_specs=[whole] * 3,
        out_specs=[far] * 3,
        scratch_shapes=[dma((3,))],
        compiler_params=pltpu.CompilerParams(vmem_limit_bytes=8 * 1024 * 1024),
    )(*[pltpu.with_memory_space_constraint(a, vm) for a in outs])
    return gt[None], gw[None], gr


def solution(mesh, plane=PLANE, cols=COLUMNS):
    placed = (
        P(("expert", "replica"), None, None),
        P(),
        P("expert", None, "replica"),
        P("expert", "replica", None),
        P(("expert", "replica"), None, None),
    )
    return jax.shard_map(
        functools.partial(body, plane, cols),
        mesh=mesh,
        in_specs=placed,
        out_specs=(
            P(("expert", "replica"), None, None),
            P("expert", "replica", None),
            P("expert", None),
        ),
        check_vma=False,
    )
```

```python
import functools

import jax
import jax.numpy as jnp
from jax import lax
from jax.experimental import pallas as pl
from jax.experimental.pallas import tpu as pltpu
from jax.sharding import PartitionSpec as P

F32 = jnp.float32
BF16 = jnp.bfloat16
MESH = pl.DeviceIdType.MESH
PLANE = 16
COLUMNS = 256


def matmul(a, b):
    return jnp.dot(a, b, preferred_element_type=F32)


def matmul_nt(a, b):
    return lax.dot_general(a, b, (((1,), (1,)), ((), ())), preferred_element_type=F32)


def matmul_tn(a, b):
    return lax.dot_general(a, b, (((0,), (0,)), ((), ())), preferred_element_type=F32)


def softmax(logits, axis):
    raised = jnp.exp(logits - jnp.max(logits, axis=axis, keepdims=True))
    return raised / jnp.sum(raised, axis=axis, keepdims=True)


def kernel(
    nz, np_, share, cols, pad, tall,
    tok_hbm, rt_hbm, win_hbm, wout_hbm, cot_hbm,
    gt, gw, gr,
    tok, rt, win, wout, cot, tok_p,
    disp, comb, disp_t, comb_t, through, grad_c, grad_d,
    slots, gathered, bundles, arrived, partial, partials, sent_back, returned,
    regroup, regroup_t, xa, xb, slope, hid, gpre, grad_rows,
    rsend, rall, rpart, rfin,
    load_sem, fz_s, fz_r, fp_s, fp_r, bp_s, bp_r, bz_s, bz_r, rp_s, rp_r, rf_s, rf_r,
):
    e = lax.axis_index("expert")
    r = lax.axis_index("replica")
    z = lax.div(e, np_)
    p = lax.rem(e, np_)
    nq = 2 * np_
    q = r * np_ + p
    experts = nz * np_
    span = 2 * nz
    wide = 2 * np_
    width = tok.shape[1]
    inner = hid.shape[1]
    chunks = width // cols
    half = cols // 2
    step = inner // chunks
    tiles = chunks
    upper = nz // 2

    def below(value, limit):
        return lax.bitwise_and(value, jnp.int32(limit - 1))

    def z_peer(k):
        far = (k + 1) // 2
        return below(z + (far if k % 2 else nz - far), nz)

    def plane_peer(k):
        return below(q + k, nq)

    def plane_device(other):
        return (z * np_ + below(other, np_), lax.div(other, np_))

    loads = [
        pltpu.make_async_copy(src, dst, load_sem.at[i])
        for i, (src, dst) in enumerate(
            ((tok_hbm, tok), (rt_hbm, rt), (cot_hbm, cot), (win_hbm, win), (wout_hbm, wout)))
    ]
    for load in loads:
        load.start()

    barrier = pltpu.get_barrier_semaphore()

    for k in range(1, nz):
        other = z_peer(k) * np_ + p
        pl.semaphore_signal(barrier, inc=1, device_id=(other, r), device_id_type=MESH)
        pl.semaphore_signal(barrier, inc=1, device_id=(other, 1 - r), device_id_type=MESH)

    for k in range(1, nq):
        pl.semaphore_signal(
            barrier, inc=1, device_id=plane_device(plane_peer(k)), device_id_type=MESH)

    def z_send(src, dst, s, t):
        for k in range(1, nz):
            other = z_peer(k)
            pltpu.make_async_remote_copy(
                src_ref=src.at[other], dst_ref=dst.at[z], send_sem=s, recv_sem=t,
                device_id=(other * np_ + p, r), device_id_type=MESH).start()
        dst[z] = src[z]

    def plane_send(src, dst, s, t, fold):
        for k in range(1, nq):
            other = plane_peer(k)
            pltpu.make_async_remote_copy(
                src_ref=src.at[below(other, np_) if fold else other], dst_ref=dst.at[q],
                send_sem=s, recv_sem=t, device_id=plane_device(other),
                device_id_type=MESH).start()
        dst[q] = src[p if fold else q]

    def all_of(ref, count, s, t):
        part = ref.at[pl.ds(0, count)]
        return pltpu.make_async_remote_copy(
            src_ref=part, dst_ref=part, send_sem=s, recv_sem=t,
            device_id=plane_device(plane_peer(1)), device_id_type=MESH)

    def columns(c):
        return pl.ds(pl.multiple_of(c * cols, cols), cols)

    def hidden_units(t):
        return pl.ds(pl.multiple_of(t * step, step), step)

    grad_c[...] = jnp.zeros_like(grad_c)
    grad_d[...] = jnp.zeros_like(grad_d)
    loads[0].wait()
    loads[1].wait()
    logits = matmul(tok[...], rt[...])
    dispatch = softmax(logits, 0)
    disp[...] = dispatch
    disp_t[...] = dispatch.T.astype(BF16)
    pl.semaphore_wait(barrier, 2 * (nz - 1) + nq - 1)

    def slot_rows(c, weights, values):
        out = matmul(weights[...], values).astype(BF16)
        slots[c, :, :np_, :] = out[:, :half].reshape(nz, np_, half)
        slots[c, :, np_:, :] = out[:, half:].reshape(nz, np_, half)
        z_send(slots.at[c], gathered.at[c], fz_s.at[c], fz_r.at[c])

    @pl.loop(0, chunks)
    def _(c):
        slot_rows(c, disp_t, tok[:, columns(c)])

    combine = softmax(logits, 1)
    comb[...] = combine
    comb_t[...] = combine.T.astype(BF16)
    loads[2].wait()

    @pl.loop(0, chunks)
    def _(c):
        slot_rows(chunks + c, comb_t, cot[:, columns(c)])

    at_row = lax.broadcasted_iota(jnp.int32, (np_ * span, nz * wide), 0)
    at_col = lax.broadcasted_iota(jnp.int32, (np_ * span, nz * wide), 1)
    inside = lax.rem(at_col, wide)
    regroup[...] = jnp.where(
        at_row == lax.rem(inside, np_) * span + lax.div(inside, np_) * nz
        + lax.div(at_col, wide), 1.0, 0.0).astype(BF16)
    inside = lax.rem(at_row, wide)
    regroup_t[...] = jnp.where(
        at_col == lax.rem(inside, np_) * span + lax.div(inside, np_) * nz
        + lax.div(at_row, wide), 1.0, 0.0).astype(BF16)

    def gateway(c):
        all_of(gathered.at[c], nz - 1, fz_s.at[c], fz_r.at[c]).wait_recv()
        bundles[c] = matmul(
            regroup[...], gathered[c].reshape(nz * wide, half)
        ).astype(BF16).reshape(np_, span, half)
        plane_send(bundles.at[c], arrived.at[c], fp_s.at[c], fp_r.at[c], True)

    many = tok_p.shape[0] // 4

    def spread_tokens(t):
        row = lax.broadcasted_iota(jnp.int32, (many, width), 0) + t * many
        col = lax.broadcasted_iota(jnp.int32, (many, width), 1)
        to = lax.div(row, tall)
        row = row - to * tall
        level = jnp.zeros_like(row)
        for k in range(1, upper):
            level = level + jnp.where(row >= k * share, 1, 0)
        level_r = lax.div(to, np_)
        source = (
            (level_r * upper + level) * (np_ * share) + (to - level_r * np_) * share
            + row - level * share)
        pick = jnp.where((col == source) & (row < upper * share), 1.0, 0.0).astype(BF16)
        tok_p[pl.ds(pl.multiple_of(t * many, many), many), :] = matmul_nt(
            pick, tok[...]).astype(BF16)

    def expert_rows(c):
        all_of(arrived.at[c], nq - 1, fp_s.at[c], fp_r.at[c]).wait_recv()
        block = arrived[c].astype(F32)
        return jnp.concatenate(
            [block[:, :nz, :].reshape(nq * nz, half), block[:, nz:, :].reshape(nq * nz, half)],
            axis=1).astype(BF16)

    def add_input(c):
        xa[:, columns(c)] = expert_rows(c)

    def add_grad(c):
        xb[:, columns(c)] = expert_rows(chunks + c)

    def forward_units(t):
        at = hidden_units(t)
        act = matmul(xa[...], win[:, at])
        lower = 0.5 * (1.0 + lax.erf(act * 0.7071067811865476))
        hid[:, at] = (act * lower).astype(BF16)
        slope[:, at] = lower + act * jnp.exp(-0.5 * act * act) * 0.3989422804014327

    def backward_units(t):
        at = hidden_units(t)
        gpre[:, at] = (matmul_nt(xb[...], wout[at, :]) * slope[:, at]).astype(BF16)

    def send_back(c, out):
        partial[c] = jnp.concatenate(
            [out[:, :half].reshape(nq, nz, half), out[:, half:].reshape(nq, nz, half)],
            axis=1).astype(BF16)
        plane_send(partial.at[c], partials.at[c], bp_s.at[c], bp_r.at[c], False)

    def send_out(c):
        send_back(c, matmul(hid[...], wout[:, columns(c)]))

    def send_grad(c):
        send_back(chunks + c, matmul_nt(gpre[...], win[columns(c), :]))

    def gateway_back(c):
        all_of(partials.at[c], nq - 1, bp_s.at[c], bp_r.at[c]).wait_recv()
        both = (partials[c, :np_].astype(F32) + partials[c, np_:].astype(F32)).astype(BF16)
        sent_back[c] = matmul(
            regroup_t[...], both.reshape(np_ * span, half)
        ).astype(BF16).reshape(nz, wide, half)
        z_send(sent_back.at[c], returned.at[c], bz_s.at[c], bz_r.at[c])

    def image_rows(c):
        all_of(returned.at[c], nz - 1, bz_s.at[c], bz_r.at[c]).wait_recv()
        block = returned[c]
        return jnp.concatenate(
            [block[:, :np_, :].reshape(experts, half), block[:, np_:, :].reshape(experts, half)],
            axis=1)

    def image_out(c):
        grad_c[...] += matmul_nt(cot[:, columns(c)], image_rows(c))

    def image_grad(c):
        rows = image_rows(chunks + c)
        grad_rows[:, columns(c)] = rows
        grad_d[...] += matmul_nt(tok[:, columns(c)], rows)

    def weight_rows(t):
        at = hidden_units(t)
        gw[at, :] = matmul_tn(hid[:, at], xb[...]).astype(BF16)

    def forward_sent(c):
        all_of(slots.at[c], nz - 1, fz_s.at[c], fz_r.at[c]).wait_send()
        all_of(arrived.at[c], nq - 1, fp_s.at[c], fp_r.at[c]).wait_send()

    def backward_sent(c):
        all_of(partials.at[c], nq - 1, bp_s.at[c], bp_r.at[c]).wait_send()
        all_of(returned.at[c], nz - 1, bz_s.at[c], bz_r.at[c]).wait_send()

    lag = min(3, chunks - 1)

    @pl.loop(0, lag)
    def _(c):
        gateway(c)
        spread_tokens(c)

    for t in range(lag, 4):
        spread_tokens(t)

    @pl.loop(lag, lag + chunks)
    def _(c):
        gateway(c)
        add_input(c - lag)

    loads[3].wait()
    loads[4].wait()
    early = chunks - lag
    first = -(-tiles // early)

    @pl.loop(0, early)
    def _(c):
        @pl.loop(c * first, jnp.minimum((c + 1) * first, tiles))
        def _(t):
            forward_units(t)

        gateway(lag + chunks + c)

    @pl.loop(0, chunks)
    def _(c):
        send_out(c)
        add_grad(c)

    @pl.loop(0, tiles)
    def _(t):
        backward_units(t)

    @pl.loop(0, chunks)
    def _(c):
        send_grad(c)
        gateway_back(c)

    @pl.loop(0, chunks)
    def _(c):
        weight_rows(c)
        forward_sent(c)
        forward_sent(chunks + c)
        image_out(c)
        gateway_back(chunks + c)

    got = grad_c[...]
    weight = comb[...]
    through[...] = weight * (got - jnp.sum(weight * got, axis=1, keepdims=True))

    @pl.loop(0, chunks)
    def _(c):
        image_grad(c)

    got = grad_d[...]
    weight = disp[...]
    grad_logits = (
        weight * (got - jnp.sum(weight * got, axis=0, keepdims=True)) + through[...]
    ).astype(BF16)
    rsend[...] = matmul(tok_p[...], grad_logits).astype(BF16).reshape(rsend.shape)
    plane_send(rsend, rall, rp_s, rp_r, False)
    gt[...] = (
        matmul(weight.astype(BF16), grad_rows[...]) + matmul_nt(grad_logits, rt[...])
    ).astype(BF16)

    @pl.loop(0, 2 * chunks)
    def _(c):
        backward_sent(c)

    at_row = lax.broadcasted_iota(jnp.int32, (upper * pad, tall), 0)
    at_col = lax.broadcasted_iota(jnp.int32, (upper * pad, tall), 1)
    level = lax.div(at_row, pad)
    own = at_row - level * pad
    place = jnp.where(
        (at_col == level * share + own) & (own < share), 1.0, 0.0).astype(BF16)
    all_of(rall, nq - 1, rp_s, rp_r).wait_recv()
    group = jnp.sum(rall[...].astype(F32), axis=0).astype(BF16)
    rpart[...] = matmul(place, group).astype(BF16).reshape(rpart.shape)
    mine = lax.div(z, upper)

    def hand_over(t):
        level, other = lax.div(t, 2), lax.rem(t, 2)
        to = r * upper + level
        copy = pltpu.make_async_remote_copy(
            src_ref=rpart.at[level], dst_ref=rfin.at[z], send_sem=rf_s.at[t],
            recv_sem=rf_r.at[z], device_id=(to * np_ + p, other), device_id_type=MESH)
        return copy, (to != z) | (other != r)

    @pl.loop(0, nz)
    def _(t):
        copy, away = hand_over(t)

        @pl.when(away)
        def _():
            copy.start()

        @pl.when(jnp.logical_not(away))
        def _():
            rfin[z] = rpart[lax.div(t, 2)]

    @pl.loop(0, nz)
    def _(k):
        @pl.when((k != z) | (mine != r))
        def _():
            pltpu.make_async_remote_copy(
                src_ref=rpart.at[0], dst_ref=rfin.at[k], send_sem=rf_s.at[0],
                recv_sem=rf_r.at[k], device_id=plane_device(plane_peer(1)),
                device_id_type=MESH).wait_recv()

    gr[...] = jnp.sum(rfin[...].astype(F32), axis=0)[:share]
    all_of(rsend, nq - 1, rp_s, rp_r).wait_send()

    @pl.loop(0, nz)
    def _(t):
        copy, away = hand_over(t)

        @pl.when(away)
        def _():
            copy.wait_send()


def write_out(gt, gw, gr, gt_hbm, gw_hbm, gr_hbm, sem):
    moves = [
        pltpu.make_async_copy(src, dst, sem.at[i])
        for i, (src, dst) in enumerate(((gw, gw_hbm), (gt, gt_hbm), (gr, gr_hbm)))
    ]
    for move in moves:
        move.start()
    for move in moves:
        move.wait()


def body(np_, cols, tokens, router, w_in, w_out, cotangent):
    count, width = tokens.shape[1:]
    experts = router.shape[1]
    inner = w_in.shape[2]
    nz = experts // np_
    nq = 2 * np_
    span = 2 * nz
    wide = 2 * np_
    share = width // experts
    pad = -(-share // 16) * 16
    tall = -(-share * (nz // 2) // 16) * 16
    parts = 2 * (width // cols)
    half = cols // 2
    vm = pltpu.VMEM
    dma = pltpu.SemaphoreType.DMA
    whole = pl.BlockSpec(memory_space=vm)
    far = pl.BlockSpec(memory_space=pltpu.HBM)
    operands = [
        pltpu.with_memory_space_constraint(a, pltpu.HBM)
        for a in (tokens[0], router, w_in[0], w_out[0], cotangent[0])
    ]
    outs = pl.pallas_call(
        functools.partial(kernel, nz, np_, share, cols, pad, tall),
        out_shape=(vm((count, width), BF16), vm((inner, width), BF16), vm((share, experts), F32)),
        in_specs=[far] * 5,
        out_specs=(whole, whole, whole),
        scratch_shapes=[
            vm((count, width), BF16), vm(router.shape, BF16), vm((width, inner), BF16),
            vm((inner, width), BF16), vm((count, width), BF16), vm((nq * tall, count), BF16),
            vm((count, experts), F32), vm((count, experts), F32),
            vm((experts, count), BF16), vm((experts, count), BF16), vm((count, experts), F32),
            vm((count, experts), F32), vm((count, experts), F32),
            vm((parts, nz, wide, half), BF16), vm((parts, nz, wide, half), BF16),
            vm((parts, np_, span, half), BF16), vm((parts, nq, span, half), BF16),
            vm((parts, nq, span, half), BF16), vm((parts, nq, span, half), BF16),
            vm((parts, nz, wide, half), BF16), vm((parts, nz, wide, half), BF16),
            vm((np_ * span, nz * wide), BF16), vm((nz * wide, np_ * span), BF16),
            vm((nq * nz, width), BF16), vm((nq * nz, width), BF16), vm((nq * nz, inner), F32),
            vm((nq * nz, inner), BF16), vm((nq * nz, inner), BF16), vm((experts, width), BF16),
            vm((nq, tall, experts), BF16), vm((nq, tall, experts), BF16),
            vm((nz // 2, pad, experts), BF16), vm((nz, pad, experts), BF16),
            dma((5,)), dma((parts,)), dma((parts,)), dma((parts,)), dma((parts,)),
            dma((parts,)), dma((parts,)), dma((parts,)), dma((parts,)),
            dma(()), dma(()), dma((nz,)), dma((nz,)),
        ],
        compiler_params=pltpu.CompilerParams(
            collective_id=0, has_side_effects=True, vmem_limit_bytes=48 * 1024 * 1024),
    )(*operands)
    gt, gw, gr = pl.pallas_call(
        write_out,
        out_shape=[jax.ShapeDtypeStruct(a.shape, a.dtype) for a in outs],
        in_specs=[whole] * 3,
        out_specs=[far] * 3,
        scratch_shapes=[dma((3,))],
        compiler_params=pltpu.CompilerParams(vmem_limit_bytes=8 * 1024 * 1024),
    )(*[pltpu.with_memory_space_constraint(a, vm) for a in outs])
    return gt[None], gw[None], gr


def solution(mesh, plane=PLANE, cols=COLUMNS):
    placed = (
        P(("expert", "replica"), None, None),
        P(),
        P("expert", None, "replica"),
        P("expert", "replica", None),
        P(("expert", "replica"), None, None),
    )
    return jax.shard_map(
        functools.partial(body, plane, cols),
        mesh=mesh,
        in_specs=placed,
        out_specs=(
            P(("expert", "replica"), None, None),
            P("expert", "replica", None),
            P("expert", None),
        ),
        check_vma=False,
    )
```

```python
import functools

import jax
import jax.numpy as jnp
from jax import lax
from jax.experimental import pallas as pl
from jax.experimental.pallas import tpu as pltpu
from jax.sharding import PartitionSpec as P

F32 = jnp.float32
BF16 = jnp.bfloat16
MESH = pl.DeviceIdType.MESH
PLANE = 16
COLUMNS = 256


def matmul(a, b):
    return jnp.dot(a, b, preferred_element_type=F32)


def matmul_nt(a, b):
    return lax.dot_general(a, b, (((1,), (1,)), ((), ())), preferred_element_type=F32)


def matmul_tn(a, b):
    return lax.dot_general(a, b, (((0,), (0,)), ((), ())), preferred_element_type=F32)


def softmax(logits, axis):
    raised = jnp.exp(logits - jnp.max(logits, axis=axis, keepdims=True))
    return raised / jnp.sum(raised, axis=axis, keepdims=True)


def kernel(
    nz, np_, share, cols, pad, tall,
    tok_hbm, rt_hbm, win_hbm, wout_hbm, cot_hbm,
    gt, gw, gr,
    tok, rt, win, wout, cot, tok_p,
    disp, comb, disp_t, comb_t, through, grad_c, grad_d,
    slots, gathered, bundles, arrived, partial, partials, sent_back, returned,
    regroup, regroup_t, xa, xb, slope, hid, gpre, grad_rows,
    rsend, rall, rpart, rfin,
    load_sem, fz_s, fz_r, fp_s, fp_r, bp_s, bp_r, bz_s, bz_r, rp_s, rp_r, rf_s, rf_r,
):
    e = lax.axis_index("expert")
    r = lax.axis_index("replica")
    z = lax.div(e, np_)
    p = lax.rem(e, np_)
    nq = 2 * np_
    q = r * np_ + p
    experts = nz * np_
    span = 2 * nz
    wide = 2 * np_
    width = tok.shape[1]
    inner = hid.shape[1]
    chunks = width // cols
    half = cols // 2
    step = inner // chunks
    tiles = chunks
    upper = nz // 2

    def below(value, limit):
        return lax.bitwise_and(value, jnp.int32(limit - 1))

    def hops(step, size):
        return min(step, size - step)

    ring = sorted(range(1, nz), key=lambda step: -hops(step, nz))
    rows_y = np_ // 4
    steps = sorted(
        [(a, b, c) for a in range(4) for b in range(rows_y) for c in range(2)][1:],
        key=lambda step: -(hops(step[0], 4) + hops(step[1], rows_y)))
    my_x = 2 * lax.div(p, 2 * rows_y) + r
    my_y = below(lax.div(p, 2), rows_y)
    my_core = below(p, 2)

    def z_peer(k):
        return below(z + ring[k - 1], nz)

    def plane_peer(k):
        a, b, c = steps[k - 1]
        to_x, to_y, to_core = below(my_x + a, 4), below(my_y + b, rows_y), below(my_core + c, 2)
        return below(to_x, 2) * np_ + (lax.div(to_x, 2) * rows_y + to_y) * 2 + to_core

    def plane_device(other):
        return (z * np_ + below(other, np_), lax.div(other, np_))

    loads = [
        pltpu.make_async_copy(src, dst, load_sem.at[i])
        for i, (src, dst) in enumerate(
            ((tok_hbm, tok), (rt_hbm, rt), (cot_hbm, cot), (win_hbm, win), (wout_hbm, wout)))
    ]
    for load in loads:
        load.start()

    barrier = pltpu.get_barrier_semaphore()

    for k in range(1, nz):
        other = z_peer(k) * np_ + p
        pl.semaphore_signal(barrier, inc=1, device_id=(other, r), device_id_type=MESH)
        pl.semaphore_signal(barrier, inc=1, device_id=(other, 1 - r), device_id_type=MESH)

    for k in range(1, nq):
        pl.semaphore_signal(
            barrier, inc=1, device_id=plane_device(plane_peer(k)), device_id_type=MESH)

    def z_send(src, dst, s, t):
        for k in range(1, nz):
            other = z_peer(k)
            pltpu.make_async_remote_copy(
                src_ref=src.at[other], dst_ref=dst.at[z], send_sem=s, recv_sem=t,
                device_id=(other * np_ + p, r), device_id_type=MESH).start()
        dst[z] = src[z]

    def plane_send(src, dst, s, t, fold):
        for k in range(1, nq):
            other = plane_peer(k)
            pltpu.make_async_remote_copy(
                src_ref=src.at[below(other, np_) if fold else other], dst_ref=dst.at[q],
                send_sem=s, recv_sem=t, device_id=plane_device(other),
                device_id_type=MESH).start()
        dst[q] = src[p if fold else q]

    def all_of(ref, count, s, t):
        part = ref.at[pl.ds(0, count)]
        return pltpu.make_async_remote_copy(
            src_ref=part, dst_ref=part, send_sem=s, recv_sem=t,
            device_id=plane_device(plane_peer(1)), device_id_type=MESH)

    def columns(c):
        return pl.ds(pl.multiple_of(c * cols, cols), cols)

    def hidden_units(t):
        return pl.ds(pl.multiple_of(t * step, step), step)

    grad_c[...] = jnp.zeros_like(grad_c)
    grad_d[...] = jnp.zeros_like(grad_d)
    loads[0].wait()
    loads[1].wait()
    logits = matmul(tok[...], rt[...])
    dispatch = softmax(logits, 0)
    disp[...] = dispatch
    disp_t[...] = dispatch.T.astype(BF16)
    pl.semaphore_wait(barrier, 2 * (nz - 1) + nq - 1)

    def slot_rows(c, weights, values):
        out = matmul(weights[...], values).astype(BF16)
        slots[c, :, :np_, :] = out[:, :half].reshape(nz, np_, half)
        slots[c, :, np_:, :] = out[:, half:].reshape(nz, np_, half)
        z_send(slots.at[c], gathered.at[c], fz_s.at[c], fz_r.at[c])

    @pl.loop(0, chunks)
    def _(c):
        slot_rows(c, disp_t, tok[:, columns(c)])

    combine = softmax(logits, 1)
    comb[...] = combine
    comb_t[...] = combine.T.astype(BF16)
    loads[2].wait()

    @pl.loop(0, chunks)
    def _(c):
        slot_rows(chunks + c, comb_t, cot[:, columns(c)])

    at_row = lax.broadcasted_iota(jnp.int32, (np_ * span, nz * wide), 0)
    at_col = lax.broadcasted_iota(jnp.int32, (np_ * span, nz * wide), 1)
    inside = lax.rem(at_col, wide)
    regroup[...] = jnp.where(
        at_row == lax.rem(inside, np_) * span + lax.div(inside, np_) * nz
        + lax.div(at_col, wide), 1.0, 0.0).astype(BF16)
    inside = lax.rem(at_row, wide)
    regroup_t[...] = jnp.where(
        at_col == lax.rem(inside, np_) * span + lax.div(inside, np_) * nz
        + lax.div(at_row, wide), 1.0, 0.0).astype(BF16)

    def gateway(c):
        all_of(gathered.at[c], nz - 1, fz_s.at[c], fz_r.at[c]).wait_recv()
        bundles[c] = matmul(
            regroup[...], gathered[c].reshape(nz * wide, half)
        ).astype(BF16).reshape(np_, span, half)
        plane_send(bundles.at[c], arrived.at[c], fp_s.at[c], fp_r.at[c], True)

    many = tok_p.shape[0] // 4

    def spread_tokens(t):
        row = lax.broadcasted_iota(jnp.int32, (many, width), 0) + t * many
        col = lax.broadcasted_iota(jnp.int32, (many, width), 1)
        to = lax.div(row, tall)
        row = row - to * tall
        level = jnp.zeros_like(row)
        for k in range(1, upper):
            level = level + jnp.where(row >= k * share, 1, 0)
        level_r = lax.div(to, np_)
        source = (
            (level_r * upper + level) * (np_ * share) + (to - level_r * np_) * share
            + row - level * share)
        pick = jnp.where((col == source) & (row < upper * share), 1.0, 0.0).astype(BF16)
        tok_p[pl.ds(pl.multiple_of(t * many, many), many), :] = matmul_nt(
            pick, tok[...]).astype(BF16)

    def expert_rows(c):
        all_of(arrived.at[c], nq - 1, fp_s.at[c], fp_r.at[c]).wait_recv()
        block = arrived[c].astype(F32)
        return jnp.concatenate(
            [block[:, :nz, :].reshape(nq * nz, half), block[:, nz:, :].reshape(nq * nz, half)],
            axis=1).astype(BF16)

    def add_input(c):
        xa[:, columns(c)] = expert_rows(c)

    def add_grad(c):
        xb[:, columns(c)] = expert_rows(chunks + c)

    def forward_units(t):
        at = hidden_units(t)
        act = matmul(xa[...], win[:, at])
        lower = 0.5 * (1.0 + lax.erf(act * 0.7071067811865476))
        hid[:, at] = (act * lower).astype(BF16)
        slope[:, at] = lower + act * jnp.exp(-0.5 * act * act) * 0.3989422804014327

    def backward_units(t):
        at = hidden_units(t)
        gpre[:, at] = (matmul_nt(xb[...], wout[at, :]) * slope[:, at]).astype(BF16)

    def send_back(c, out):
        partial[c] = jnp.concatenate(
            [out[:, :half].reshape(nq, nz, half), out[:, half:].reshape(nq, nz, half)],
            axis=1).astype(BF16)
        plane_send(partial.at[c], partials.at[c], bp_s.at[c], bp_r.at[c], False)

    def send_out(c):
        send_back(c, matmul(hid[...], wout[:, columns(c)]))

    def send_grad(c):
        send_back(chunks + c, matmul_nt(gpre[...], win[columns(c), :]))

    def gateway_back(c):
        all_of(partials.at[c], nq - 1, bp_s.at[c], bp_r.at[c]).wait_recv()
        both = (partials[c, :np_].astype(F32) + partials[c, np_:].astype(F32)).astype(BF16)
        sent_back[c] = matmul(
            regroup_t[...], both.reshape(np_ * span, half)
        ).astype(BF16).reshape(nz, wide, half)
        z_send(sent_back.at[c], returned.at[c], bz_s.at[c], bz_r.at[c])

    def image_rows(c):
        all_of(returned.at[c], nz - 1, bz_s.at[c], bz_r.at[c]).wait_recv()
        block = returned[c]
        return jnp.concatenate(
            [block[:, :np_, :].reshape(experts, half), block[:, np_:, :].reshape(experts, half)],
            axis=1)

    def image_out(c):
        grad_c[...] += matmul_nt(cot[:, columns(c)], image_rows(c))

    def image_grad(c):
        rows = image_rows(chunks + c)
        grad_rows[:, columns(c)] = rows
        grad_d[...] += matmul_nt(tok[:, columns(c)], rows)

    def weight_rows(t):
        at = hidden_units(t)
        gw[at, :] = matmul_tn(hid[:, at], xb[...]).astype(BF16)

    def forward_sent(c):
        all_of(slots.at[c], nz - 1, fz_s.at[c], fz_r.at[c]).wait_send()
        all_of(arrived.at[c], nq - 1, fp_s.at[c], fp_r.at[c]).wait_send()

    def backward_sent(c):
        all_of(partials.at[c], nq - 1, bp_s.at[c], bp_r.at[c]).wait_send()
        all_of(returned.at[c], nz - 1, bz_s.at[c], bz_r.at[c]).wait_send()

    lag = min(3, chunks - 1)

    @pl.loop(0, lag)
    def _(c):
        gateway(c)
        spread_tokens(c)

    for t in range(lag, 4):
        spread_tokens(t)

    @pl.loop(lag, lag + chunks)
    def _(c):
        gateway(c)
        add_input(c - lag)

    loads[3].wait()
    loads[4].wait()
    early = chunks - lag
    first = -(-tiles // early)

    @pl.loop(0, early)
    def _(c):
        @pl.loop(c * first, jnp.minimum((c + 1) * first, tiles))
        def _(t):
            forward_units(t)

        gateway(lag + chunks + c)

    @pl.loop(0, chunks)
    def _(c):
        send_out(c)
        add_grad(c)

    @pl.loop(0, tiles)
    def _(t):
        backward_units(t)

    @pl.loop(0, chunks)
    def _(c):
        send_grad(c)
        gateway_back(c)

    @pl.loop(0, chunks)
    def _(c):
        weight_rows(c)
        forward_sent(c)
        forward_sent(chunks + c)
        image_out(c)
        gateway_back(chunks + c)

    got = grad_c[...]
    weight = comb[...]
    through[...] = weight * (got - jnp.sum(weight * got, axis=1, keepdims=True))

    @pl.loop(0, chunks)
    def _(c):
        image_grad(c)

    got = grad_d[...]
    weight = disp[...]
    grad_logits = (
        weight * (got - jnp.sum(weight * got, axis=0, keepdims=True)) + through[...]
    ).astype(BF16)
    rsend[...] = matmul(tok_p[...], grad_logits).astype(BF16).reshape(rsend.shape)
    plane_send(rsend, rall, rp_s, rp_r, False)
    gt[...] = (
        matmul(weight.astype(BF16), grad_rows[...]) + matmul_nt(grad_logits, rt[...])
    ).astype(BF16)

    @pl.loop(0, 2 * chunks)
    def _(c):
        backward_sent(c)

    at_row = lax.broadcasted_iota(jnp.int32, (upper * pad, tall), 0)
    at_col = lax.broadcasted_iota(jnp.int32, (upper * pad, tall), 1)
    level = lax.div(at_row, pad)
    own = at_row - level * pad
    place = jnp.where(
        (at_col == level * share + own) & (own < share), 1.0, 0.0).astype(BF16)
    all_of(rall, nq - 1, rp_s, rp_r).wait_recv()
    group = jnp.sum(rall[...].astype(F32), axis=0).astype(BF16)
    rpart[...] = matmul(place, group).astype(BF16).reshape(rpart.shape)
    mine = lax.div(z, upper)

    def hand_over(t):
        level, other = lax.div(t, 2), lax.rem(t, 2)
        to = r * upper + level
        copy = pltpu.make_async_remote_copy(
            src_ref=rpart.at[level], dst_ref=rfin.at[z], send_sem=rf_s.at[t],
            recv_sem=rf_r.at[z], device_id=(to * np_ + p, other), device_id_type=MESH)
        return copy, (to != z) | (other != r)

    @pl.loop(0, nz)
    def _(t):
        copy, away = hand_over(t)

        @pl.when(away)
        def _():
            copy.start()

        @pl.when(jnp.logical_not(away))
        def _():
            rfin[z] = rpart[lax.div(t, 2)]

    @pl.loop(0, nz)
    def _(k):
        @pl.when((k != z) | (mine != r))
        def _():
            pltpu.make_async_remote_copy(
                src_ref=rpart.at[0], dst_ref=rfin.at[k], send_sem=rf_s.at[0],
                recv_sem=rf_r.at[k], device_id=plane_device(plane_peer(1)),
                device_id_type=MESH).wait_recv()

    gr[...] = jnp.sum(rfin[...].astype(F32), axis=0)[:share]
    all_of(rsend, nq - 1, rp_s, rp_r).wait_send()

    @pl.loop(0, nz)
    def _(t):
        copy, away = hand_over(t)

        @pl.when(away)
        def _():
            copy.wait_send()


def write_out(gt, gw, gr, gt_hbm, gw_hbm, gr_hbm, sem):
    moves = [
        pltpu.make_async_copy(src, dst, sem.at[i])
        for i, (src, dst) in enumerate(((gw, gw_hbm), (gt, gt_hbm), (gr, gr_hbm)))
    ]
    for move in moves:
        move.start()
    for move in moves:
        move.wait()


def body(np_, cols, tokens, router, w_in, w_out, cotangent):
    count, width = tokens.shape[1:]
    experts = router.shape[1]
    inner = w_in.shape[2]
    nz = experts // np_
    nq = 2 * np_
    span = 2 * nz
    wide = 2 * np_
    share = width // experts
    pad = -(-share // 16) * 16
    tall = -(-share * (nz // 2) // 16) * 16
    parts = 2 * (width // cols)
    half = cols // 2
    vm = pltpu.VMEM
    dma = pltpu.SemaphoreType.DMA
    whole = pl.BlockSpec(memory_space=vm)
    far = pl.BlockSpec(memory_space=pltpu.HBM)
    operands = [
        pltpu.with_memory_space_constraint(a, pltpu.HBM)
        for a in (tokens[0], router, w_in[0], w_out[0], cotangent[0])
    ]
    outs = pl.pallas_call(
        functools.partial(kernel, nz, np_, share, cols, pad, tall),
        out_shape=(vm((count, width), BF16), vm((inner, width), BF16), vm((share, experts), F32)),
        in_specs=[far] * 5,
        out_specs=(whole, whole, whole),
        scratch_shapes=[
            vm((count, width), BF16), vm(router.shape, BF16), vm((width, inner), BF16),
            vm((inner, width), BF16), vm((count, width), BF16), vm((nq * tall, count), BF16),
            vm((count, experts), F32), vm((count, experts), F32),
            vm((experts, count), BF16), vm((experts, count), BF16), vm((count, experts), F32),
            vm((count, experts), F32), vm((count, experts), F32),
            vm((parts, nz, wide, half), BF16), vm((parts, nz, wide, half), BF16),
            vm((parts, np_, span, half), BF16), vm((parts, nq, span, half), BF16),
            vm((parts, nq, span, half), BF16), vm((parts, nq, span, half), BF16),
            vm((parts, nz, wide, half), BF16), vm((parts, nz, wide, half), BF16),
            vm((np_ * span, nz * wide), BF16), vm((nz * wide, np_ * span), BF16),
            vm((nq * nz, width), BF16), vm((nq * nz, width), BF16), vm((nq * nz, inner), F32),
            vm((nq * nz, inner), BF16), vm((nq * nz, inner), BF16), vm((experts, width), BF16),
            vm((nq, tall, experts), BF16), vm((nq, tall, experts), BF16),
            vm((nz // 2, pad, experts), BF16), vm((nz, pad, experts), BF16),
            dma((5,)), dma((parts,)), dma((parts,)), dma((parts,)), dma((parts,)),
            dma((parts,)), dma((parts,)), dma((parts,)), dma((parts,)),
            dma(()), dma(()), dma((nz,)), dma((nz,)),
        ],
        compiler_params=pltpu.CompilerParams(
            collective_id=0, has_side_effects=True, vmem_limit_bytes=48 * 1024 * 1024),
    )(*operands)
    gt, gw, gr = pl.pallas_call(
        write_out,
        out_shape=[jax.ShapeDtypeStruct(a.shape, a.dtype) for a in outs],
        in_specs=[whole] * 3,
        out_specs=[far] * 3,
        scratch_shapes=[dma((3,))],
        compiler_params=pltpu.CompilerParams(vmem_limit_bytes=8 * 1024 * 1024),
    )(*[pltpu.with_memory_space_constraint(a, vm) for a in outs])
    return gt[None], gw[None], gr


def solution(mesh, plane=PLANE, cols=COLUMNS):
    placed = (
        P(("expert", "replica"), None, None),
        P(),
        P("expert", None, "replica"),
        P("expert", "replica", None),
        P(("expert", "replica"), None, None),
    )
    return jax.shard_map(
        functools.partial(body, plane, cols),
        mesh=mesh,
        in_specs=placed,
        out_specs=(
            P(("expert", "replica"), None, None),
            P("expert", "replica", None),
            P("expert", None),
        ),
        check_vma=False,
    )
```

```python
import functools

import jax
import jax.numpy as jnp
from jax import lax
from jax.experimental import pallas as pl
from jax.experimental.pallas import tpu as pltpu
from jax.sharding import PartitionSpec as P

F32 = jnp.float32
BF16 = jnp.bfloat16
MESH = pl.DeviceIdType.MESH
PLANE = 16
COLUMNS = 256


def matmul(a, b):
    return jnp.dot(a, b, preferred_element_type=F32)


def matmul_nt(a, b):
    return lax.dot_general(a, b, (((1,), (1,)), ((), ())), preferred_element_type=F32)


def matmul_tn(a, b):
    return lax.dot_general(a, b, (((0,), (0,)), ((), ())), preferred_element_type=F32)


def softmax(logits, axis):
    raised = jnp.exp(logits - jnp.max(logits, axis=axis, keepdims=True))
    return raised / jnp.sum(raised, axis=axis, keepdims=True)


def kernel(
    nz, np_, share, cols, pad, tall,
    tok_hbm, rt_hbm, win_hbm, wout_hbm, cot_hbm,
    gt, gw, gr,
    tok, rt, win, wout, cot, tok_p,
    disp, comb, disp_t, comb_t, through, grad_c, grad_d,
    slots, gathered, bundles, arrived, partial, partials, sent_back, returned,
    regroup, regroup_t, xa, xb, slope, hid, gpre, grad_rows,
    rsend, rall, rpart, rfin,
    load_sem, fz_s, fz_r, fp_s, fp_r, bp_s, bp_r, bz_s, bz_r, rp_s, rp_r, rf_s, rf_r,
):
    e = lax.axis_index("expert")
    r = lax.axis_index("replica")
    z = lax.div(e, np_)
    p = lax.rem(e, np_)
    nq = 2 * np_
    q = r * np_ + p
    experts = nz * np_
    span = 2 * nz
    wide = 2 * np_
    width = tok.shape[1]
    inner = hid.shape[1]
    chunks = width // cols
    half = cols // 2
    step = inner // chunks
    tiles = chunks
    upper = nz // 2

    def below(value, limit):
        return lax.bitwise_and(value, jnp.int32(limit - 1))

    def hops(step, size):
        return min(step, size - step)

    ring = sorted(range(1, nz), key=lambda step: -hops(step, nz))
    rows_y = np_ // 4
    steps = sorted(
        [(a, b, c) for a in range(4) for b in range(rows_y) for c in range(2)][1:],
        key=lambda step: -(hops(step[0], 4) + hops(step[1], rows_y)))
    my_x = 2 * lax.div(p, 2 * rows_y) + r
    my_y = below(lax.div(p, 2), rows_y)
    my_core = below(p, 2)

    def z_peer(k):
        return below(z + ring[k - 1], nz)

    def plane_peer(k):
        a, b, c = steps[k - 1]
        to_x, to_y, to_core = below(my_x + a, 4), below(my_y + b, rows_y), below(my_core + c, 2)
        return below(to_x, 2) * np_ + (lax.div(to_x, 2) * rows_y + to_y) * 2 + to_core

    def plane_device(other):
        return (z * np_ + below(other, np_), lax.div(other, np_))

    loads = [
        pltpu.make_async_copy(src, dst, load_sem.at[i])
        for i, (src, dst) in enumerate(
            ((tok_hbm, tok), (rt_hbm, rt), (cot_hbm, cot), (win_hbm, win), (wout_hbm, wout)))
    ]
    for load in loads:
        load.start()

    barrier = pltpu.get_barrier_semaphore()

    for k in range(1, nz):
        other = z_peer(k) * np_ + p
        pl.semaphore_signal(barrier, inc=1, device_id=(other, r), device_id_type=MESH)
        pl.semaphore_signal(barrier, inc=1, device_id=(other, 1 - r), device_id_type=MESH)

    for k in range(1, nq):
        pl.semaphore_signal(
            barrier, inc=1, device_id=plane_device(plane_peer(k)), device_id_type=MESH)

    def z_send(src, dst, s, t):
        for k in range(1, nz):
            other = z_peer(k)
            pltpu.make_async_remote_copy(
                src_ref=src.at[other], dst_ref=dst.at[z], send_sem=s, recv_sem=t,
                device_id=(other * np_ + p, r), device_id_type=MESH).start()
        dst[z] = src[z]

    def plane_send(src, dst, s, t, fold):
        for k in range(1, nq):
            other = plane_peer(k)
            pltpu.make_async_remote_copy(
                src_ref=src.at[below(other, np_) if fold else other], dst_ref=dst.at[q],
                send_sem=s, recv_sem=t, device_id=plane_device(other),
                device_id_type=MESH).start()
        dst[q] = src[p if fold else q]

    def all_of(ref, count, s, t):
        part = ref.at[pl.ds(0, count)]
        return pltpu.make_async_remote_copy(
            src_ref=part, dst_ref=part, send_sem=s, recv_sem=t,
            device_id=plane_device(plane_peer(1)), device_id_type=MESH)

    def columns(c):
        return pl.ds(pl.multiple_of(c * cols, cols), cols)

    def hidden_units(t):
        return pl.ds(pl.multiple_of(t * step, step), step)

    grad_c[...] = jnp.zeros_like(grad_c)
    grad_d[...] = jnp.zeros_like(grad_d)
    loads[0].wait()
    loads[1].wait()
    logits = matmul(tok[...], rt[...])
    dispatch = softmax(logits, 0)
    disp[...] = dispatch
    disp_t[...] = dispatch.T.astype(BF16)
    pl.semaphore_wait(barrier, 2 * (nz - 1) + nq - 1)

    def slot_rows(c, weights, values):
        out = matmul(weights[...], values).astype(BF16)
        slots[c, :, :np_, :] = out[:, :half].reshape(nz, np_, half)
        slots[c, :, np_:, :] = out[:, half:].reshape(nz, np_, half)
        z_send(slots.at[c], gathered.at[c], fz_s.at[c], fz_r.at[c])

    @pl.loop(0, chunks)
    def _(c):
        slot_rows(c, disp_t, tok[:, columns(c)])

    combine = softmax(logits, 1)
    comb[...] = combine
    comb_t[...] = combine.T.astype(BF16)
    loads[2].wait()

    @pl.loop(0, chunks)
    def _(c):
        slot_rows(chunks + c, comb_t, cot[:, columns(c)])

    at_row = lax.broadcasted_iota(jnp.int32, (np_ * span, nz * wide), 0)
    at_col = lax.broadcasted_iota(jnp.int32, (np_ * span, nz * wide), 1)
    inside = lax.rem(at_col, wide)
    regroup[...] = jnp.where(
        at_row == lax.rem(inside, np_) * span + lax.div(inside, np_) * nz
        + lax.div(at_col, wide), 1.0, 0.0).astype(BF16)
    inside = lax.rem(at_row, wide)
    regroup_t[...] = jnp.where(
        at_col == lax.rem(inside, np_) * span + lax.div(inside, np_) * nz
        + lax.div(at_row, wide), 1.0, 0.0).astype(BF16)

    def gateway(c):
        all_of(gathered.at[c], nz - 1, fz_s.at[c], fz_r.at[c]).wait_recv()
        bundles[c] = matmul(
            regroup[...], gathered[c].reshape(nz * wide, half)
        ).astype(BF16).reshape(np_, span, half)
        plane_send(bundles.at[c], arrived.at[c], fp_s.at[c], fp_r.at[c], True)

    many = tok_p.shape[0] // 4

    def spread_tokens(t):
        row = lax.broadcasted_iota(jnp.int32, (many, width), 0) + t * many
        col = lax.broadcasted_iota(jnp.int32, (many, width), 1)
        to = lax.div(row, tall)
        row = row - to * tall
        level = jnp.zeros_like(row)
        for k in range(1, upper):
            level = level + jnp.where(row >= k * share, 1, 0)
        level_r = lax.div(to, np_)
        source = (
            (level_r * upper + level) * (np_ * share) + (to - level_r * np_) * share
            + row - level * share)
        pick = jnp.where((col == source) & (row < upper * share), 1.0, 0.0).astype(BF16)
        tok_p[pl.ds(pl.multiple_of(t * many, many), many), :] = matmul_nt(
            pick, tok[...]).astype(BF16)

    def expert_rows(c):
        all_of(arrived.at[c], nq - 1, fp_s.at[c], fp_r.at[c]).wait_recv()
        block = arrived[c].astype(F32)
        return jnp.concatenate(
            [block[:, :nz, :].reshape(nq * nz, half), block[:, nz:, :].reshape(nq * nz, half)],
            axis=1).astype(BF16)

    def add_input(c):
        xa[:, columns(c)] = expert_rows(c)

    def add_grad(c):
        xb[:, columns(c)] = expert_rows(chunks + c)

    def forward_units(t):
        at = hidden_units(t)
        act = matmul(xa[...], win[:, at])
        lower = 0.5 * (1.0 + lax.erf(act * 0.7071067811865476))
        hid[:, at] = (act * lower).astype(BF16)
        slope[:, at] = lower + act * jnp.exp(-0.5 * act * act) * 0.3989422804014327

    def backward_units(t):
        at = hidden_units(t)
        gpre[:, at] = (matmul_nt(xb[...], wout[at, :]) * slope[:, at]).astype(BF16)

    def send_back(c, out):
        partial[c] = jnp.concatenate(
            [out[:, :half].reshape(nq, nz, half), out[:, half:].reshape(nq, nz, half)],
            axis=1).astype(BF16)
        plane_send(partial.at[c], partials.at[c], bp_s.at[c], bp_r.at[c], False)

    def send_out(c):
        send_back(c, matmul(hid[...], wout[:, columns(c)]))

    def send_grad(c):
        send_back(chunks + c, matmul_nt(gpre[...], win[columns(c), :]))

    def gateway_back(c):
        all_of(partials.at[c], nq - 1, bp_s.at[c], bp_r.at[c]).wait_recv()
        both = (partials[c, :np_].astype(F32) + partials[c, np_:].astype(F32)).astype(BF16)
        sent_back[c] = matmul(
            regroup_t[...], both.reshape(np_ * span, half)
        ).astype(BF16).reshape(nz, wide, half)
        z_send(sent_back.at[c], returned.at[c], bz_s.at[c], bz_r.at[c])

    def image_rows(c):
        all_of(returned.at[c], nz - 1, bz_s.at[c], bz_r.at[c]).wait_recv()
        block = returned[c]
        return jnp.concatenate(
            [block[:, :np_, :].reshape(experts, half), block[:, np_:, :].reshape(experts, half)],
            axis=1)

    def image_out(c):
        grad_c[...] += matmul_nt(cot[:, columns(c)], image_rows(c))

    def image_grad(c):
        rows = image_rows(chunks + c)
        grad_rows[:, columns(c)] = rows
        grad_d[...] += matmul_nt(tok[:, columns(c)], rows)

    def weight_rows(t):
        at = hidden_units(t)
        gw[at, :] = matmul_tn(hid[:, at], xb[...]).astype(BF16)

    def forward_sent(c):
        all_of(slots.at[c], nz - 1, fz_s.at[c], fz_r.at[c]).wait_send()
        all_of(arrived.at[c], nq - 1, fp_s.at[c], fp_r.at[c]).wait_send()

    def backward_sent(c):
        all_of(partials.at[c], nq - 1, bp_s.at[c], bp_r.at[c]).wait_send()
        all_of(returned.at[c], nz - 1, bz_s.at[c], bz_r.at[c]).wait_send()

    lag = min(3, chunks - 1)

    @pl.loop(0, lag)
    def _(c):
        gateway(c)
        spread_tokens(c)

    for t in range(lag, 4):
        spread_tokens(t)

    @pl.loop(lag, lag + chunks)
    def _(c):
        gateway(c)
        add_input(c - lag)

    loads[3].wait()
    loads[4].wait()
    early = chunks - lag
    first = -(-tiles // early)

    @pl.loop(0, early)
    def _(c):
        @pl.loop(c * first, jnp.minimum((c + 1) * first, tiles))
        def _(t):
            forward_units(t)

        gateway(lag + chunks + c)

    @pl.loop(0, chunks)
    def _(c):
        send_out(c)
        add_grad(c)

    @pl.loop(0, tiles)
    def _(t):
        backward_units(t)

    @pl.loop(0, chunks)
    def _(c):
        send_grad(c)
        gateway_back(c)

    @pl.loop(0, chunks)
    def _(c):
        weight_rows(c)
        forward_sent(c)
        forward_sent(chunks + c)
        image_out(c)
        gateway_back(chunks + c)

    got = grad_c[...]
    weight = comb[...]
    through[...] = weight * (got - jnp.sum(weight * got, axis=1, keepdims=True))

    @pl.loop(0, chunks)
    def _(c):
        image_grad(c)

    got = grad_d[...]
    weight = disp[...]
    grad_logits = (
        weight * (got - jnp.sum(weight * got, axis=0, keepdims=True)) + through[...]
    ).astype(BF16)
    rsend[...] = matmul(tok_p[...], grad_logits).astype(BF16).reshape(rsend.shape)
    plane_send(rsend, rall, rp_s, rp_r, False)
    gt[...] = (
        matmul(weight.astype(BF16), grad_rows[...]) + matmul_nt(grad_logits, rt[...])
    ).astype(BF16)

    @pl.loop(0, 2 * chunks)
    def _(c):
        backward_sent(c)

    at_row = lax.broadcasted_iota(jnp.int32, (upper * pad, tall), 0)
    at_col = lax.broadcasted_iota(jnp.int32, (upper * pad, tall), 1)
    level = lax.div(at_row, pad)
    own = at_row - level * pad
    place = jnp.where(
        (at_col == level * share + own) & (own < share), 1.0, 0.0).astype(BF16)
    all_of(rall, nq - 1, rp_s, rp_r).wait_recv()
    group = jnp.sum(rall[...].astype(F32), axis=0).astype(BF16)
    rpart[...] = matmul(place, group).astype(BF16).reshape(rpart.shape)
    mine = lax.div(z, upper)

    def hand_over(t):
        level, other = t // 2, t % 2
        to = r * upper + level
        copy = pltpu.make_async_remote_copy(
            src_ref=rpart.at[level], dst_ref=rfin.at[z], send_sem=rf_s.at[t],
            recv_sem=rf_r.at[z], device_id=(to * np_ + p, other), device_id_type=MESH)
        return copy, (to != z) | (other != r)

    for t in range(nz):
        copy, away = hand_over(t)
        pl.when(away)(copy.start)

    @pl.when(mine == r)
    def _():
        rfin[z] = rpart[below(z, upper)]

    for k in range(nz):
        @pl.when((k != z) | (mine != r))
        def _():
            pltpu.make_async_remote_copy(
                src_ref=rpart.at[0], dst_ref=rfin.at[k], send_sem=rf_s.at[0],
                recv_sem=rf_r.at[k], device_id=plane_device(plane_peer(1)),
                device_id_type=MESH).wait_recv()

    gr[...] = jnp.sum(rfin[...].astype(F32), axis=0)[:share]
    all_of(rsend, nq - 1, rp_s, rp_r).wait_send()

    for t in range(nz):
        copy, away = hand_over(t)
        pl.when(away)(copy.wait_send)


def write_out(gt, gw, gr, gt_hbm, gw_hbm, gr_hbm, sem):
    moves = [
        pltpu.make_async_copy(src, dst, sem.at[i])
        for i, (src, dst) in enumerate(((gw, gw_hbm), (gt, gt_hbm), (gr, gr_hbm)))
    ]
    for move in moves:
        move.start()
    for move in moves:
        move.wait()


def body(np_, cols, tokens, router, w_in, w_out, cotangent):
    count, width = tokens.shape[1:]
    experts = router.shape[1]
    inner = w_in.shape[2]
    nz = experts // np_
    nq = 2 * np_
    span = 2 * nz
    wide = 2 * np_
    share = width // experts
    pad = -(-share // 16) * 16
    tall = -(-share * (nz // 2) // 16) * 16
    parts = 2 * (width // cols)
    half = cols // 2
    vm = pltpu.VMEM
    dma = pltpu.SemaphoreType.DMA
    whole = pl.BlockSpec(memory_space=vm)
    far = pl.BlockSpec(memory_space=pltpu.HBM)
    operands = [
        pltpu.with_memory_space_constraint(a, pltpu.HBM)
        for a in (tokens[0], router, w_in[0], w_out[0], cotangent[0])
    ]
    outs = pl.pallas_call(
        functools.partial(kernel, nz, np_, share, cols, pad, tall),
        out_shape=(vm((count, width), BF16), vm((inner, width), BF16), vm((share, experts), F32)),
        in_specs=[far] * 5,
        out_specs=(whole, whole, whole),
        scratch_shapes=[
            vm((count, width), BF16), vm(router.shape, BF16), vm((width, inner), BF16),
            vm((inner, width), BF16), vm((count, width), BF16), vm((nq * tall, count), BF16),
            vm((count, experts), F32), vm((count, experts), F32),
            vm((experts, count), BF16), vm((experts, count), BF16), vm((count, experts), F32),
            vm((count, experts), F32), vm((count, experts), F32),
            vm((parts, nz, wide, half), BF16), vm((parts, nz, wide, half), BF16),
            vm((parts, np_, span, half), BF16), vm((parts, nq, span, half), BF16),
            vm((parts, nq, span, half), BF16), vm((parts, nq, span, half), BF16),
            vm((parts, nz, wide, half), BF16), vm((parts, nz, wide, half), BF16),
            vm((np_ * span, nz * wide), BF16), vm((nz * wide, np_ * span), BF16),
            vm((nq * nz, width), BF16), vm((nq * nz, width), BF16), vm((nq * nz, inner), F32),
            vm((nq * nz, inner), BF16), vm((nq * nz, inner), BF16), vm((experts, width), BF16),
            vm((nq, tall, experts), BF16), vm((nq, tall, experts), BF16),
            vm((nz // 2, pad, experts), BF16), vm((nz, pad, experts), BF16),
            dma((5,)), dma((parts,)), dma((parts,)), dma((parts,)), dma((parts,)),
            dma((parts,)), dma((parts,)), dma((parts,)), dma((parts,)),
            dma(()), dma(()), dma((nz,)), dma((nz,)),
        ],
        compiler_params=pltpu.CompilerParams(
            collective_id=0, has_side_effects=True, vmem_limit_bytes=48 * 1024 * 1024),
    )(*operands)
    gt, gw, gr = pl.pallas_call(
        write_out,
        out_shape=[jax.ShapeDtypeStruct(a.shape, a.dtype) for a in outs],
        in_specs=[whole] * 3,
        out_specs=[far] * 3,
        scratch_shapes=[dma((3,))],
        compiler_params=pltpu.CompilerParams(vmem_limit_bytes=8 * 1024 * 1024),
    )(*[pltpu.with_memory_space_constraint(a, vm) for a in outs])
    return gt[None], gw[None], gr


def solution(mesh, plane=PLANE, cols=COLUMNS):
    placed = (
        P(("expert", "replica"), None, None),
        P(),
        P("expert", None, "replica"),
        P("expert", "replica", None),
        P(("expert", "replica"), None, None),
    )
    return jax.shard_map(
        functools.partial(body, plane, cols),
        mesh=mesh,
        in_specs=placed,
        out_specs=(
            P(("expert", "replica"), None, None),
            P("expert", "replica", None),
            P("expert", None),
        ),
        check_vma=False,
    )
```
